256 devices in a mesh: rep: 64 (over z, y, x_hi), fsdp: 4 (over x_lo, core).
Axes of the slice: x: 4 (x_hi: 2, x_lo: 2; x = x_hi * 2 + x_lo), y: 4, z: 8, core: 2. Of those that a mesh axis runs over, the one named last changes fastest.
Arguments:
- hidden_in: bfloat16 [65536, 8192], P(('rep', 'fsdp')), may hold values from -6 to 6
- norm_gain: float32 [8192], replicated, may hold values from 0.5 to 1.5
- key_weight: bfloat16 [64, 8192, 512], P('rep', 'fsdp'), may hold values from -0.0625 to 0.0625
- key_cot: bfloat16 [65536, 512], P(('rep', 'fsdp')), may hold values from -3 to 3
- global_base: float32 [6144, 128], P('fsdp'), may hold values from -2 to 2, as said below
- replica_params: bfloat16 [64, 6144, 128], P('rep', 'fsdp'), may hold values from -2.25 to 2.25, as said below
- outer_momentum: float32 [6144, 128], P('fsdp'), may hold values from -2 to 2
- scale_exponents: int32 [6144], P('fsdp'), may hold values from -6 to -2
- dither_seeds: int32 [64, 6144], P('rep', 'fsdp'), may hold values from 0 to 1048575
- fragment_index: int32 [1], replicated, may hold values from 0 to 32748
Outputs:
- keys: bfloat16 [65536, 512], P(('rep', 'fsdp'))
- weight_grad: bfloat16 [64, 8192, 512], P('rep', 'fsdp')
- input_grad: bfloat16 [65536, 8192], P(('rep', 'fsdp'))
- new_base: float32 [6144, 128], P('fsdp')
- new_momentum: float32 [6144, 128], P('fsdp')
The draws below stay inside these ranges and needn't reach their ends.
Inputs may be any that keep to these rules, and one draw needn't show every extreme that they name: `global_base`: every entry's magnitude lies between 0.25 and 2, and it is a bfloat16 value. `replica_params`: each entry has the sign of the same entry of global_base and differs from it by at most 0.25.
All inputs are finite; a program needn't handle non-finite values.
Results may differ from the reference program's by a relative error of at most 0.0034.
The reference program's roundings to bfloat16 on the way (of `normed`) count: a program that leaves them out, or rounds other values in their place, can miss the bound.
Values may be sent and summed in bfloat16 or wider, within the bound.
No kernel may reach another device: no remote copies, remote signals or barrier semaphores. Data moves between devices by JAX's collectives and lax.ppermute only.
A program may use at most 128 MiB of HBM per device.

```python
import math
import jax
import jax.numpy as jnp
from jax import lax

D = 8192
LANES = 128
TOK_DEV = 256
KW = 512
REPS = 64
TOKENS = 65536
FRAG_ROWS = 6144
N_REP = 64
N_FSDP = 4


def shared_base(key):
    sign_key, size_key = jax.random.split(key)
    shape = (FRAG_ROWS, LANES)
    signs = jnp.where(jax.random.bernoulli(sign_key, 0.5, shape), jnp.float32(1.0), jnp.float32(-1.0))
    magnitude = jnp.exp(jax.random.uniform(size_key, shape, jnp.float32, math.log(0.25), math.log(2.0)))
    return (signs * magnitude).astype(jnp.bfloat16).astype(jnp.float32)


def draw_global_base(key, part):
    return shared_base(key)


def draw_replica_params(key, part):
    base = shared_base(key)
    key = jax.random.fold_in(key, 12)
    shape = (REPS, FRAG_ROWS, LANES)
    noise = jnp.clip(0.08 * jax.random.normal(key, shape, jnp.float32), -0.24, 0.24)
    return (base[None, :, :] + noise).astype(jnp.bfloat16)


def plant(entries, stream_key, least, largest):
    longest = entries.shape.index(max(entries.shape))
    spots = []
    for shift in (0, 1):
        where = [jax.random.randint(jax.random.fold_in(stream_key, axis), (), 0, length) for axis, length in enumerate(entries.shape)]
        where[longest] = (where[longest] + shift) % entries.shape[longest]
        spots.append(tuple(where))
    return entries.at[spots[0]].set(least).at[spots[1]].set(largest)


def block_scale(key, dims, cuts, low, high):
    level = 1.0
    for dim, shards_of in cuts:
        heights = jax.random.uniform(jax.random.fold_in(jax.random.fold_in(key, 6), dim), (shards_of,), jnp.float32, low / len(cuts), high / len(cuts))
        level = level * jnp.repeat(jnp.exp(heights), dims[dim] // shards_of).reshape((-1,) + (1,) * (len(dims) - 1 - dim))
    return level


def gaussian(stream_key, dims, spread, reach, cuts=(), kind=jnp.bfloat16):
    values = jax.random.normal(stream_key, dims, jnp.float32) * spread
    if len(cuts) > 0:
        values = block_scale(stream_key, dims, cuts, -0.22, 0.18) * values
    return jnp.clip(values, min=-reach, max=reach).astype(kind)


def setup_inputs(seed: int = 0) -> dict:
    key_of = jax.random.split(jax.random.key(seed), 11)
    hidden_in = gaussian(key_of[0], (TOKENS, D), 1.0, 6.0, ((0, 256),))
    norm_gain = jnp.clip(1.0 + 0.1 * jax.random.normal(key_of[1], (D,), jnp.float32), 0.5, 1.5)
    key_weight = gaussian(key_of[2], (REPS, D, KW), D ** -0.5, 0.0625, ((0, 64), (1, 4)))
    key_cot = gaussian(key_of[3], (TOKENS, KW), 0.5, 3.0, ((0, 256),))
    global_base = draw_global_base(jax.random.fold_in(key_of[10], 71), 0)
    replica_params = draw_replica_params(jax.random.fold_in(key_of[10], 71), 0)
    outer_momentum = gaussian(key_of[6], (FRAG_ROWS, LANES), 0.3, 2.0, ((0, 4),), jnp.float32)
    scale_exponents = plant(jax.random.randint(key_of[7], (FRAG_ROWS,), -6, -1), jax.random.fold_in(key_of[7], 1), -6, (-1) - 1).astype(jnp.int32)
    dither_seeds = plant(jax.random.randint(key_of[8], (REPS, FRAG_ROWS), 0, 1048576), jax.random.fold_in(key_of[8], 1), 0, 1048575).astype(jnp.int32)
    fragment_index = jax.random.randint(key_of[9], (1,), 0, 32749).astype(jnp.int32)
    return {"hidden_in": hidden_in, "norm_gain": norm_gain, "key_weight": key_weight, "key_cot": key_cot, "global_base": global_base, "replica_params": replica_params, "outer_momentum": outer_momentum, "scale_exponents": scale_exponents, "dither_seeds": dither_seeds, "fragment_index": fragment_index}


eps_norm = 1e-05
momentum_keep = 0.9
outer_rate = 0.7

def level_table(exponents):
    powers = jnp.arange(-6, -1, dtype=jnp.int32)
    values = jnp.array([64.0, 32.0, 16.0, 8.0, 4.0], dtype=jnp.float32)
    match = exponents[:, None] == powers[None, :]
    return lax.optimization_barrier(jnp.sum(jnp.where(match, values[None, :], jnp.float32(0.0)), axis=1))

def dither_levels(seeds, fragment, lanes):
    lane = jnp.arange(lanes, dtype=jnp.int32)
    first = (seeds[:, None] + 7919 * lane[None, :] + 4099 * fragment) % 32749
    second = (first * first + 3 * first + 17) % 32749
    return second % 16

def reference(hidden_in, norm_gain, key_weight, key_cot, global_base, replica_params, outer_momentum, scale_exponents, dither_seeds, fragment_index):
    per_rep = N_FSDP * TOK_DEV
    width = key_weight.shape[2]

    def run_replica(items):
        tokens, weight, cot = items
        values = tokens.astype(jnp.float32)
        inv_rms = lax.rsqrt(lax.optimization_barrier(jnp.mean(values * values, axis=1, keepdims=True)) + eps_norm)
        normed = (values * inv_rms * norm_gain).astype(jnp.bfloat16)
        keys = jnp.dot(normed, weight, preferred_element_type=jnp.float32).astype(jnp.bfloat16)
        grad = jnp.dot(normed.T, cot, preferred_element_type=jnp.float32).astype(jnp.bfloat16)
        dnormed = jnp.dot(cot, weight.T, preferred_element_type=jnp.float32)
        scaled = norm_gain * dnormed
        inner = lax.optimization_barrier(jnp.sum(scaled * values, axis=1, keepdims=True)) / D
        cubed = inv_rms * inv_rms * inv_rms
        dinput = (inv_rms * scaled - values * cubed * inner).astype(jnp.bfloat16)
        return (keys, grad, dinput)
    tokens_all = hidden_in.reshape(N_REP, per_rep, D)
    cots_all = key_cot.reshape(N_REP, per_rep, width)
    keys, weight_grad, input_grad = lax.map(run_replica, (tokens_all, key_weight, cots_all))
    keys = keys.reshape(N_REP * per_rep, width)
    input_grad = input_grad.reshape(N_REP * per_rep, D)
    level = level_table(scale_exponents)[:, None]
    step_size = 1.0 / level
    fragment = fragment_index[0]
    lanes = global_base.shape[1]

    def add_codes(total, items):
        params, seeds = items
        delta = global_base - params.astype(jnp.float32)
        offset = (dither_levels(seeds, fragment, lanes).astype(jnp.float32) + 0.5) / 16.0
        code = jnp.clip(jnp.floor(delta * level + offset), -8.0, 7.0).astype(jnp.int32)
        return (total + code, None)
    start = jnp.zeros(global_base.shape, dtype=jnp.int32)
    code_sum, unused = lax.scan(add_codes, start, (replica_params, dither_seeds))
    outer_grad = code_sum.astype(jnp.float32) * (step_size / N_REP)
    new_momentum = momentum_keep * outer_momentum + outer_grad
    new_base = global_base - outer_rate * (outer_grad + momentum_keep * new_momentum)
    return (keys, weight_grad, input_grad, new_base, new_momentum)
```

```python
import functools

import jax
import jax.numpy as jnp
from jax import lax
from jax.experimental import pallas as pl
from jax.experimental.pallas import tpu as pltpu
from jax.sharding import PartitionSpec as P

eps_norm = 1e-05
momentum_keep = 0.9
outer_rate = 0.7
axes = ("rep", "fsdp")
f32 = jnp.float32
bf16 = jnp.bfloat16
cuts = (0, 1536, 2048)
small = pl.CostEstimate(flops=1024, bytes_accessed=1024, transcendentals=0)


def flip(bit):
    return [(i, i ^ bit) for i in range(256)]


core_bit, x_lo_bit, x_hi_bit, y_bit, z_bit = 1, 2, 4, 8, 32


def send(value, bit):
    return lax.ppermute(value, axes, flip(bit))


def params(limit=58):
    return pltpu.CompilerParams(vmem_limit_bytes=limit * 1024 * 1024)


def level_table(exponents):
    powers = jnp.arange(-6, -1, dtype=jnp.int32)
    values = jnp.array([64.0, 32.0, 16.0, 8.0, 4.0], dtype=jnp.float32)
    match = exponents[:, None] == powers[None, :]
    return jnp.sum(jnp.where(match, values[None, :], jnp.float32(0.0)), axis=1)


def dither_levels(seeds, fragment, lanes):
    lane = jnp.arange(lanes, dtype=jnp.int32)
    first = (seeds[:, None] + 7919 * lane[None, :] + 4099 * fragment) % 32749
    second = (first * first + 3 * first + 17) % 32749
    return second % 16


def norm_kernel(me_ref, x_ref, gain_ref, near_ref, f0_ref, f1_ref, f2_ref, f3_ref, inv_ref):
    width = x_ref.shape[1]
    slab = width // 4
    half = slab // 2
    total = jnp.zeros((x_ref.shape[0], 1), f32)
    for s in range(4):
        part = x_ref[:, s * slab : (s + 1) * slab].astype(f32)
        total = total + jnp.sum(part * part, axis=1, keepdims=True)
    inv = lax.rsqrt(total / width + eps_norm)
    inv_ref[...] = jnp.broadcast_to(inv, inv_ref.shape)
    me = me_ref[0]

    def normed(bits, offset, count):
        col = pl.multiple_of((me ^ bits) * slab + offset, half)
        part = x_ref[:, pl.ds(col, count)].astype(f32)
        return (part * inv * gain_ref[:, pl.ds(col, count)]).astype(bf16)

    near_ref[0] = normed(0, 0, slab)
    near_ref[1] = normed(2, 0, slab)
    f0_ref[...] = normed(1, 0, half)
    f1_ref[...] = normed(1, half, half)
    f2_ref[...] = normed(3, 0, half)
    f3_ref[...] = normed(3, half, half)


def norm_slabs(me, hidden, gain):
    rows, width = hidden.shape
    block = 64
    slab = width // 4
    near, *far, inv = pl.pallas_call(
        norm_kernel,
        grid_spec=pltpu.PrefetchScalarGridSpec(
            num_scalar_prefetch=1,
            grid=(rows // block,),
            in_specs=[
                pl.BlockSpec((block, width), lambda i, m: (i, 0)),
                pl.BlockSpec((1, width), lambda i, m: (0, 0)),
            ],
            out_specs=[pl.BlockSpec((2, block, slab), lambda i, m: (0, i, 0))]
            + [pl.BlockSpec((block, slab // 2), lambda i, m: (i, 0))] * 4
            + [pl.BlockSpec((block, 128), lambda i, m: (i, 0))],
        ),
        out_shape=[pltpu.HBM((2, rows, slab), bf16)]
        + [pltpu.HBM((rows, slab // 2), bf16)] * 4
        + [jax.ShapeDtypeStruct((rows, 128), f32)],
        compiler_params=params(),
        cost_estimate=small,
        name="norm",
    )(me, hidden, gain)
    return near, far, inv


def grad_kernel(mine_ref, low_ref, high_ref, cot_ref, cot_theirs_ref, *out_refs):
    over_tokens = (((0,), (0,)), ((), ()))
    step = 512
    half = low_ref.shape[1]
    for first, last, out_ref in zip(cuts, cuts[1:], out_refs):
        for row in range(first, last, step):
            theirs_ref = low_ref if row < half else high_ref
            a = mine_ref[0, :, row : row + step]
            b = theirs_ref[:, row % half : row % half + step]
            value = lax.dot_general(a, cot_ref[...], over_tokens, preferred_element_type=f32)
            value = value + lax.dot_general(b, cot_theirs_ref[...], over_tokens, preferred_element_type=f32)
            out_ref[row - first : row - first + step, :] = value.astype(out_ref.dtype)


def grad_rows(mine, theirs, cot, cot_theirs, place, dtype, name):
    _, tokens, slab = mine.shape
    width = cot.shape[1]
    counts = [b - a for a, b in zip(cuts, cuts[1:])]
    fixed = lambda i: (0, 0)
    return pl.pallas_call(
        grad_kernel,
        grid=(1,),
        in_specs=[
            pl.BlockSpec((1, tokens, slab), lambda i: (place, 0, 0)),
            pl.BlockSpec((tokens, slab // 2), fixed),
            pl.BlockSpec((tokens, slab // 2), fixed),
            pl.BlockSpec((tokens, width), fixed),
            pl.BlockSpec((tokens, width), fixed),
        ],
        out_specs=[pl.BlockSpec((rows, width), fixed) for rows in counts],
        out_shape=[pltpu.HBM((rows, width), dtype) for rows in counts],
        compiler_params=params(),
        cost_estimate=small,
        name=name,
    )(mine, theirs[2 * place], theirs[2 * place + 1], cot, cot_theirs)


def add_kernel(own_ref, came_ref, *refs):
    refs[-1][0] = (own_ref[...] + came_ref[...].astype(f32)).astype(bf16)


def add_rows(own, came, first, so_far):
    rows, width = own.shape
    block = 512
    part = pl.BlockSpec((block, width), lambda g: (g, 0))
    args = (own, came) if so_far is None else (own, came, so_far)
    return pl.pallas_call(
        add_kernel,
        grid=(rows // block,),
        in_specs=[part, part] + ([] if so_far is None else [pl.BlockSpec(memory_space=pl.ANY)]),
        out_specs=pl.BlockSpec((1, block, width), lambda g: (0, first // block + g, 0)),
        out_shape=jax.ShapeDtypeStruct((1, cuts[-1], width), bf16),
        input_output_aliases={} if so_far is None else {2: 0},
        compiler_params=params(),
        cost_estimate=small,
        name="add",
    )(*args)


def weight_specs(rows, block, width):
    specs = []
    first = 0
    for count in rows:
        steps = count // block

        def index(i, *_, first=first, steps=steps):
            return (jnp.clip(i - first, 0, steps - 1), 0)

        specs.append(pl.BlockSpec((block, width), index))
        first += steps
    return specs


def at_step(step, rows, block, refs, body):
    first = 0
    for count, ref in zip(rows, refs, strict=True):
        last = first + count // block

        @pl.when((step >= first) & (step < last))
        def _(ref=ref):
            body(ref)

        first = last


def keys_kernel(near_ref, *refs, rows, block, width):
    far = refs[:4]
    weights = refs[4 : 4 + len(rows)]
    cot_ref, inv_ref, keys_ref, factor_ref, total_ref = refs[4 + len(rows) :]
    step = pl.program_id(0)
    per = width // 4 // block

    @pl.when(step == 0)
    def _():
        total_ref[...] = jnp.zeros_like(total_ref)

    def near_body(w_ref):
        total_ref[...] += jnp.dot(near_ref[0], w_ref[...], preferred_element_type=f32)

    def far_body(w_ref):
        for k, part_ref in enumerate(far):

            @pl.when(step == per * (1 + 2 * (k // per)) + k % per)
            def _(part_ref=part_ref):
                total_ref[...] += jnp.dot(part_ref[...], w_ref[...], preferred_element_type=f32)

    is_near = (step // per) % 2 == 0

    @pl.when(is_near)
    def _():
        at_step(step, rows, block, weights, near_body)

    @pl.when(jnp.logical_not(is_near))
    def _():
        at_step(step, rows, block, weights, far_body)

    @pl.when(step == 4 * per - 1)
    def _():
        keys = total_ref[...]
        keys_ref[...] = keys.astype(bf16)
        dots = jnp.sum(cot_ref[...].astype(f32) * keys, axis=1, keepdims=True) / width
        inv = inv_ref[...]
        factor_ref[...] = inv * inv * dots


def keys_of(near, far, weights, cot, inv):
    _, tokens, slab = near.shape
    width = cot.shape[1]
    per = 2
    block = slab // per
    rows = [w.shape[0] for w in weights]

    def near_place(i):
        late = i >= 2 * per
        return (late.astype(jnp.int32), 0, jnp.minimum(jnp.where(late, i - 2 * per, i), per - 1))

    fixed = lambda i: (0, 0)
    return pl.pallas_call(
        functools.partial(keys_kernel, rows=rows, block=block, width=4 * slab),
        grid=(4 * per,),
        in_specs=[pl.BlockSpec((1, tokens, block), near_place)]
        + [pl.BlockSpec((tokens, block), fixed)] * 4
        + weight_specs(rows, block, width)
        + [pl.BlockSpec((tokens, width), fixed), pl.BlockSpec((tokens, 128), fixed)],
        out_specs=[pl.BlockSpec((tokens, width), fixed), pl.BlockSpec((tokens, 128), fixed)],
        out_shape=[jax.ShapeDtypeStruct((tokens, width), bf16), jax.ShapeDtypeStruct((tokens, 128), f32)],
        scratch_shapes=[pltpu.VMEM((tokens, width), f32)],
        compiler_params=params(),
        cost_estimate=small,
        name="keys",
    )(near, *far, *weights, cot, inv)


def input_kernel(me_ref, x_ref, gain_ref, *refs, rows, block):
    weights = refs[: len(rows)]
    cot_ref, inv_ref, factor_ref, out_ref = refs[len(rows) :]

    def body(w_ref):
        dnormed = lax.dot_general(
            cot_ref[...], w_ref[...], (((1,), (1,)), ((), ())), preferred_element_type=f32
        )
        scaled = gain_ref[...] * dnormed
        out_ref[...] = (inv_ref[:, :1] * scaled - x_ref[...].astype(f32) * factor_ref[:, :1]).astype(bf16)

    at_step(pl.program_id(0), rows, block, weights, body)


def input_grad_of(me, hidden, gain, weights, cot, inv, factor):
    tokens, total = hidden.shape
    width = cot.shape[1]
    per = 2
    block = total // 4 // per
    rows = [w.shape[0] for w in weights]

    def column(i, m):
        return (0, (m[0] ^ (i // per)) * per + i % per)

    fixed = lambda i, m: (0, 0)
    return pl.pallas_call(
        functools.partial(input_kernel, rows=rows, block=block),
        grid_spec=pltpu.PrefetchScalarGridSpec(
            num_scalar_prefetch=1,
            grid=(4 * per,),
            in_specs=[pl.BlockSpec((tokens, block), column), pl.BlockSpec((1, block), column)]
            + weight_specs(rows, block, width)
            + [
                pl.BlockSpec((tokens, width), fixed),
                pl.BlockSpec((tokens, 128), fixed),
                pl.BlockSpec((tokens, 128), fixed),
            ],
            out_specs=pl.BlockSpec((tokens, block), column),
        ),
        out_shape=jax.ShapeDtypeStruct((tokens, total), bf16),
        compiler_params=params(),
        cost_estimate=small,
        name="input_grad",
    )(me, hidden, gain, *weights, cot, inv, factor)


def packed_codes(global_base, replica_params, level, dither_seeds, fragment_index):
    rows_here, lanes = global_base.shape
    third = rows_here // 3
    delta = global_base - replica_params[0].astype(f32)
    offset = (dither_levels(dither_seeds[0], fragment_index[0], lanes).astype(f32) + 0.5) / 16.0
    code = jnp.clip(jnp.floor(delta * level + offset), -8.0, 7.0).astype(jnp.int32)
    shifted = code + 8
    return shifted[:third] + 1024 * shifted[third : 2 * third] + 1048576 * shifted[2 * third :]


def beside(got, work):
    return lax.optimization_barrier((got, work))


def halve(total, step, work):
    z = lax.axis_index("rep") // 8
    half = total.shape[0] // 2
    side = (z // step) % 2
    kept = lax.dynamic_slice_in_dim(total, side * half, half, 0)
    sent = lax.dynamic_slice_in_dim(total, (1 - side) * half, half, 0)
    got, done = beside(send(sent, z_bit * step), work())
    return kept + got, done


def exchange(total, masks, work):
    got, done = beside([send(total, mask) for mask in masks], work())
    return sum(got, total), done


def in_order(low, mine, other):
    return jnp.where(
        low, jnp.concatenate([mine, other], axis=0), jnp.concatenate([other, mine], axis=0)
    )


def rejoin_four(total, work):
    z = lax.axis_index("rep") // 8
    got, done = beside([send(total, z_bit * step) for step in (1, 2, 3)], work())
    even = z % 2 == 0
    near_pair = in_order(even, total, got[0])
    far_pair = in_order(even, got[1], got[2])
    return in_order((z // 2) % 2 == 0, near_pair, far_pair), done


def rejoin(total, step, work):
    z = lax.axis_index("rep") // 8
    other, done = beside(send(total, z_bit * step), work())
    return in_order((z // step) % 2 == 0, total, other), done


def outer_update(total, global_base, outer_momentum, level, replicas):
    step_size = 1.0 / level
    field_low = total & 1023
    field_mid = (total >> 10) & 1023
    field_high = total >> 20
    code_sum = jnp.concatenate([field_low, field_mid, field_high], axis=0) - 8 * replicas
    outer_grad = code_sum.astype(f32) * (step_size / replicas)
    new_momentum = momentum_keep * outer_momentum + outer_grad
    new_base = global_base - outer_rate * (outer_grad + momentum_keep * new_momentum)
    return (new_base, new_momentum)


def per_device(
    hidden_in,
    norm_gain,
    key_weight,
    key_cot,
    global_base,
    replica_params,
    outer_momentum,
    scale_exponents,
    dither_seeds,
    fragment_index,
):
    me = lax.axis_index("fsdp").astype(jnp.int32)[None]
    gain = norm_gain[None, :]
    own = key_weight[0]
    partner = send(own, x_lo_bit)
    sibling = send(own, core_bit)
    cot_sibling = send(key_cot, core_bit)
    nothing = lambda: ()

    level = level_table(scale_exponents)[:, None]
    total = packed_codes(global_base, replica_params, level, dither_seeds, fragment_index)
    total, hidden = lax.optimization_barrier((total, hidden_in))
    total, (near, far, inv) = halve(total, 4, lambda: norm_slabs(me, hidden, gain))
    total, came = halve(total, 2, lambda: [send(part, core_bit) for part in far])
    total, out_rows = exchange(
        total,
        (x_hi_bit | z_bit,),
        lambda: grad_rows(near, came, key_cot, cot_sibling, 1, bf16, "grad_out"),
    )
    in_rows = [send(rows, x_lo_bit) for rows in out_rows]
    total, _ = halve(total, 1, nothing)
    total, own_rows = exchange(
        total,
        (y_bit, y_bit * 2, y_bit * 3),
        lambda: grad_rows(near, came, key_cot, cot_sibling, 0, f32, "grad_own"),
    )
    total, partner = lax.optimization_barrier((total, partner))
    diagonal = send(partner, core_bit)
    total, diagonal = rejoin_four(total, lambda: diagonal)
    weights = (own, sibling, partner, diagonal)
    total, (keys, factor) = rejoin(total, 4, lambda: keys_of(near, far, weights, key_cot, inv))
    new_base, new_momentum = outer_update(
        total, global_base, outer_momentum, level, lax.axis_size("rep")
    )
    input_grad = input_grad_of(me, hidden, gain, weights, key_cot, inv, factor)
    input_grad, in_rows[0] = lax.optimization_barrier((input_grad, in_rows[0]))
    weight_grad = None
    for first, own_part, in_part in zip(cuts, own_rows, in_rows):
        weight_grad = add_rows(own_part, in_part, first, weight_grad)
    return (keys, weight_grad, input_grad, new_base, new_momentum)


def solution(mesh):
    placed = (
        P(("rep", "fsdp"), None),
        P(),
        P("rep", "fsdp", None),
        P(("rep", "fsdp"), None),
        P("fsdp", None),
        P("rep", "fsdp", None),
        P("fsdp", None),
        P("fsdp"),
        P("rep", "fsdp"),
        P(),
    )
    return jax.shard_map(
        per_device,
        mesh=mesh,
        in_specs=placed,
        out_specs=(
            P(("rep", "fsdp"), None),
            P("rep", "fsdp", None),
            P(("rep", "fsdp"), None),
            P("fsdp", None),
            P("fsdp", None),
        ),
        check_vma=False,
    )
```

```python
import functools

import jax
import jax.numpy as jnp
from jax import lax
from jax.experimental import pallas as pl
from jax.experimental.pallas import tpu as pltpu
from jax.sharding import PartitionSpec as P

eps_norm = 1e-05
momentum_keep = 0.9
outer_rate = 0.7
axes = ("rep", "fsdp")
f32 = jnp.float32
bf16 = jnp.bfloat16
cuts = (0, 1536, 2048)
small = pl.CostEstimate(flops=1024, bytes_accessed=1024, transcendentals=0)


def flip(bit):
    return [(i, i ^ bit) for i in range(256)]


core_bit, x_lo_bit, x_hi_bit, y_bit, z_bit = 1, 2, 4, 8, 32


def send(value, bit):
    return lax.ppermute(value, axes, flip(bit))


def params(limit=58):
    return pltpu.CompilerParams(vmem_limit_bytes=limit * 1024 * 1024)


def level_table(exponents):
    powers = jnp.arange(-6, -1, dtype=jnp.int32)
    values = jnp.array([64.0, 32.0, 16.0, 8.0, 4.0], dtype=jnp.float32)
    match = exponents[:, None] == powers[None, :]
    return jnp.sum(jnp.where(match, values[None, :], jnp.float32(0.0)), axis=1)


def dither_levels(seeds, fragment, lanes):
    lane = jnp.arange(lanes, dtype=jnp.int32)
    first = (seeds[:, None] + 7919 * lane[None, :] + 4099 * fragment) % 32749
    second = (first * first + 3 * first + 17) % 32749
    return second % 16


def norm_kernel(me_ref, x_ref, gain_ref, near_ref, f0_ref, f1_ref, f2_ref, f3_ref, inv_ref):
    width = x_ref.shape[1]
    slab = width // 4
    half = slab // 2
    total = jnp.zeros((x_ref.shape[0], 1), f32)
    for s in range(4):
        part = x_ref[:, s * slab : (s + 1) * slab].astype(f32)
        total = total + jnp.sum(part * part, axis=1, keepdims=True)
    inv = lax.rsqrt(total / width + eps_norm)
    inv_ref[...] = jnp.broadcast_to(inv, inv_ref.shape)
    me = me_ref[0]

    def normed(bits, offset, count):
        col = pl.multiple_of((me ^ bits) * slab + offset, half)
        part = x_ref[:, pl.ds(col, count)].astype(f32)
        return (part * inv * gain_ref[:, pl.ds(col, count)]).astype(bf16)

    near_ref[0] = normed(0, 0, slab)
    near_ref[1] = normed(2, 0, slab)
    f0_ref[...] = normed(1, 0, half)
    f1_ref[...] = normed(1, half, half)
    f2_ref[...] = normed(3, 0, half)
    f3_ref[...] = normed(3, half, half)


def norm_slabs(me, hidden, gain):
    rows, width = hidden.shape
    block = 64
    slab = width // 4
    near, *far, inv = pl.pallas_call(
        norm_kernel,
        grid_spec=pltpu.PrefetchScalarGridSpec(
            num_scalar_prefetch=1,
            grid=(rows // block,),
            in_specs=[
                pl.BlockSpec((block, width), lambda i, m: (i, 0)),
                pl.BlockSpec((1, width), lambda i, m: (0, 0)),
            ],
            out_specs=[pl.BlockSpec((2, block, slab), lambda i, m: (0, i, 0))]
            + [pl.BlockSpec((block, slab // 2), lambda i, m: (i, 0))] * 4
            + [pl.BlockSpec((block, 128), lambda i, m: (i, 0))],
        ),
        out_shape=[pltpu.HBM((2, rows, slab), bf16)]
        + [pltpu.HBM((rows, slab // 2), bf16)] * 4
        + [jax.ShapeDtypeStruct((rows, 128), f32)],
        compiler_params=params(),
        cost_estimate=small,
        name="norm",
    )(me, hidden, gain)
    return near, far, inv


def grad_kernel(mine_ref, low_ref, high_ref, cot_ref, cot_theirs_ref, *out_refs):
    over_tokens = (((0,), (0,)), ((), ()))
    step = 512
    half = low_ref.shape[1]
    for first, last, out_ref in zip(cuts, cuts[1:], out_refs):
        for row in range(first, last, step):
            theirs_ref = low_ref if row < half else high_ref
            a = mine_ref[0, :, row : row + step]
            b = theirs_ref[:, row % half : row % half + step]
            value = lax.dot_general(a, cot_ref[...], over_tokens, preferred_element_type=f32)
            value = value + lax.dot_general(b, cot_theirs_ref[...], over_tokens, preferred_element_type=f32)
            out_ref[row - first : row - first + step, :] = value.astype(out_ref.dtype)


def grad_rows(mine, theirs, cot, cot_theirs, place, dtype, name):
    _, tokens, slab = mine.shape
    width = cot.shape[1]
    counts = [b - a for a, b in zip(cuts, cuts[1:])]
    fixed = lambda i: (0, 0)
    return pl.pallas_call(
        grad_kernel,
        grid=(1,),
        in_specs=[
            pl.BlockSpec((1, tokens, slab), lambda i: (place, 0, 0)),
            pl.BlockSpec((tokens, slab // 2), fixed),
            pl.BlockSpec((tokens, slab // 2), fixed),
            pl.BlockSpec((tokens, width), fixed),
            pl.BlockSpec((tokens, width), fixed),
        ],
        out_specs=[pl.BlockSpec((rows, width), fixed) for rows in counts],
        out_shape=[pltpu.HBM((rows, width), dtype) for rows in counts],
        compiler_params=params(),
        cost_estimate=small,
        name=name,
    )(mine, theirs[2 * place], theirs[2 * place + 1], cot, cot_theirs)


def add_kernel(own_ref, came_ref, *refs):
    refs[-1][0] = (own_ref[...] + came_ref[...].astype(f32)).astype(bf16)


def add_rows(own, came, first, so_far):
    rows, width = own.shape
    block = 512
    part = pl.BlockSpec((block, width), lambda g: (g, 0))
    args = (own, came) if so_far is None else (own, came, so_far)
    return pl.pallas_call(
        add_kernel,
        grid=(rows // block,),
        in_specs=[part, part] + ([] if so_far is None else [pl.BlockSpec(memory_space=pl.ANY)]),
        out_specs=pl.BlockSpec((1, block, width), lambda g: (0, first // block + g, 0)),
        out_shape=jax.ShapeDtypeStruct((1, cuts[-1], width), bf16),
        input_output_aliases={} if so_far is None else {2: 0},
        compiler_params=params(8),
        cost_estimate=small,
        name="add",
    )(*args)


pieces = 4


def token_kernel(me_ref, near_hbm, *refs):
    far_hbm = refs[:4]
    whole_hbm = refs[4:7]
    piece_hbm = refs[7 : 7 + pieces]
    x_hbm, gain_ref, cot_ref, inv_ref, keys_ref, out_hbm = refs[7 + pieces : 13 + pieces]
    near, far, w, x, out, sems, out_sems = refs[13 + pieces :]
    _, tokens, slab = near.shape
    half = slab // 2
    width = 4 * slab
    me = me_ref[0]
    used = []

    def load(source, target):
        copy = pltpu.make_async_copy(source, target, sems.at[len(used)])
        used.append(copy)
        copy.start()
        return copy

    def column(s, h):
        return pl.multiple_of((me ^ s) * slab + h * half, half)

    waits = []
    for s in range(4):
        group = []
        if s % 2 == 0:
            group.append(load(near_hbm.at[s // 2], near.at[s // 2]))
        else:
            for k in (s - 1, s):
                group.append(load(far_hbm[k], far.at[k]))
        if s < 3:
            group.append(load(whole_hbm[s], w.at[s]))
        else:
            rows = slab // pieces
            for k in range(pieces):
                group.append(load(piece_hbm[k], w.at[s, pl.ds(k * rows, rows)]))
        waits.append(group)
    x_waits = [load(x_hbm.at[:, pl.ds(column(s, 0), slab)], x.at[s]) for s in range(4)]

    keys = jnp.zeros(keys_ref.shape, f32)
    for s in range(4):
        for copy in waits[s]:
            copy.wait()
        if s % 2 == 0:
            keys = keys + jnp.dot(near[s // 2], w[s], preferred_element_type=f32)
        else:
            for h in range(2):
                part = w[s, h * half : (h + 1) * half, :]
                keys = keys + jnp.dot(far[s - 1 + h], part, preferred_element_type=f32)
    keys_ref[...] = keys.astype(bf16)
    cot = cot_ref[...]
    inv = inv_ref[:, :1]
    factor = inv * inv * (jnp.sum(cot.astype(f32) * keys, axis=1, keepdims=True) / width)

    sent = []
    for s in range(4):
        x_waits[s].wait()
        for h in range(2):
            part = w[s, h * half : (h + 1) * half, :]
            dnormed = lax.dot_general(cot, part, (((1,), (1,)), ((), ())), preferred_element_type=f32)
            scaled = gain_ref[:, pl.ds(column(s, h), half)] * dnormed
            values = x[s, :, h * half : (h + 1) * half].astype(f32)
            out[s, h] = (inv * scaled - values * factor).astype(bf16)
            copy = pltpu.make_async_copy(
                out.at[s, h], out_hbm.at[:, pl.ds(column(s, h), half)], out_sems.at[2 * s + h]
            )
            copy.start()
            sent.append(copy)
    for copy in sent:
        copy.wait()


def token_outputs(me, near, far, whole, parts, hidden, gain, cot, inv):
    tokens, width = hidden.shape
    slab = width // 4
    keys_width = cot.shape[1]
    far_off = pl.BlockSpec(memory_space=pl.ANY)
    close = pl.BlockSpec(memory_space=pltpu.VMEM)
    loads = 2 + 4 + 3 + pieces + 4
    return pl.pallas_call(
        token_kernel,
        in_specs=[pl.BlockSpec(memory_space=pltpu.SMEM)] + [far_off] * (9 + pieces) + [close] * 3,
        out_specs=[close, far_off],
        out_shape=[
            jax.ShapeDtypeStruct((tokens, keys_width), bf16),
            jax.ShapeDtypeStruct((tokens, width), bf16),
        ],
        scratch_shapes=[
            pltpu.VMEM((2, tokens, slab), bf16),
            pltpu.VMEM((4, tokens, slab // 2), bf16),
            pltpu.VMEM((4, slab, keys_width), bf16),
            pltpu.VMEM((4, tokens, slab), bf16),
            pltpu.VMEM((4, 2, tokens, slab // 2), bf16),
            pltpu.SemaphoreType.DMA((loads,)),
            pltpu.SemaphoreType.DMA((8,)),
        ],
        compiler_params=params(),
        cost_estimate=small,
        name="keys_and_input_grad",
    )(me, near, *far, *whole, *parts, hidden, gain, cot, inv)


def split_kernel(source, *targets):
    rows = targets[0].shape[0]
    for k, target in enumerate(targets):

        @pl.when(pl.program_id(0) == k)
        def _(target=target):
            target[...] = source[...]


def in_pieces(value):
    rows, width = value.shape
    rows = rows // pieces
    return pl.pallas_call(
        split_kernel,
        grid=(pieces,),
        in_specs=[pl.BlockSpec((rows, width), lambda i: (i, 0))],
        out_specs=[pl.BlockSpec((rows, width), lambda i: (0, 0))] * pieces,
        out_shape=[pltpu.HBM((rows, width), value.dtype)] * pieces,
        compiler_params=params(),
        cost_estimate=small,
        name="split",
    )(value)


def packed_codes(global_base, replica_params, level, dither_seeds, fragment_index):
    rows_here, lanes = global_base.shape
    third = rows_here // 3
    delta = global_base - replica_params[0].astype(f32)
    offset = (dither_levels(dither_seeds[0], fragment_index[0], lanes).astype(f32) + 0.5) / 16.0
    code = jnp.clip(jnp.floor(delta * level + offset), -8.0, 7.0).astype(jnp.int32)
    shifted = code + 8
    return shifted[:third] + 1024 * shifted[third : 2 * third] + 1048576 * shifted[2 * third :]


def beside(got, work):
    return lax.optimization_barrier((got, work))


def halve(total, step, work):
    z = lax.axis_index("rep") // 8
    half = total.shape[0] // 2
    side = (z // step) % 2
    kept = lax.dynamic_slice_in_dim(total, side * half, half, 0)
    sent = lax.dynamic_slice_in_dim(total, (1 - side) * half, half, 0)
    got, done = beside(send(sent, z_bit * step), work())
    return kept + got, done


def exchange(total, masks, work):
    got, done = beside([send(total, mask) for mask in masks], work())
    return sum(got, total), done


def in_order(low, mine, other):
    return jnp.where(
        low, jnp.concatenate([mine, other], axis=0), jnp.concatenate([other, mine], axis=0)
    )


def rejoin_four(total, work):
    z = lax.axis_index("rep") // 8
    got, done = beside([send(total, z_bit * step) for step in (1, 2, 3)], work())
    even = z % 2 == 0
    near_pair = in_order(even, total, got[0])
    far_pair = in_order(even, got[1], got[2])
    return in_order((z // 2) % 2 == 0, near_pair, far_pair), done


def rejoin(total, step, work):
    z = lax.axis_index("rep") // 8
    other, done = beside(send(total, z_bit * step), work())
    return in_order((z // step) % 2 == 0, total, other), done


def outer_update(total, global_base, outer_momentum, level, replicas):
    step_size = 1.0 / level
    field_low = total & 1023
    field_mid = (total >> 10) & 1023
    field_high = total >> 20
    code_sum = jnp.concatenate([field_low, field_mid, field_high], axis=0) - 8 * replicas
    outer_grad = code_sum.astype(f32) * (step_size / replicas)
    new_momentum = momentum_keep * outer_momentum + outer_grad
    new_base = global_base - outer_rate * (outer_grad + momentum_keep * new_momentum)
    return (new_base, new_momentum)


def per_device(
    hidden_in,
    norm_gain,
    key_weight,
    key_cot,
    global_base,
    replica_params,
    outer_momentum,
    scale_exponents,
    dither_seeds,
    fragment_index,
):
    me = lax.axis_index("fsdp").astype(jnp.int32)[None]
    gain = norm_gain[None, :]
    own = key_weight[0]
    partner = send(own, x_lo_bit)
    sibling = send(own, core_bit)
    cot_sibling = send(key_cot, core_bit)
    nothing = lambda: ()

    level = level_table(scale_exponents)[:, None]
    total = packed_codes(global_base, replica_params, level, dither_seeds, fragment_index)
    total, hidden = lax.optimization_barrier((total, hidden_in))
    total, (near, far, inv) = halve(total, 4, lambda: norm_slabs(me, hidden, gain))
    total, came = halve(total, 2, lambda: [send(part, core_bit) for part in far])
    total, out_rows = exchange(
        total,
        (x_hi_bit | z_bit,),
        lambda: grad_rows(near, came, key_cot, cot_sibling, 1, bf16, "grad_out"),
    )
    in_rows = [send(rows, x_lo_bit) for rows in out_rows]
    total, _ = halve(total, 1, nothing)
    total, _ = exchange(total, (y_bit, y_bit * 2, y_bit * 3), nothing)
    total, partner = lax.optimization_barrier((total, partner))
    diagonal = [send(part, core_bit) for part in in_pieces(partner)]
    total, (diagonal, own_rows) = rejoin_four(
        total,
        lambda: (diagonal, grad_rows(near, came, key_cot, cot_sibling, 0, f32, "grad_own")),
    )
    total, (keys, input_grad) = rejoin(
        total,
        4,
        lambda: token_outputs(
            me, near, far, (own, sibling, partner), diagonal, hidden, gain, key_cot, inv
        ),
    )
    new_base, new_momentum = outer_update(
        total, global_base, outer_momentum, level, lax.axis_size("rep")
    )
    input_grad, in_rows[0] = lax.optimization_barrier((input_grad, in_rows[0]))
    weight_grad = None
    for first, own_part, in_part in zip(cuts, own_rows, in_rows):
        weight_grad = add_rows(own_part, in_part, first, weight_grad)
    return (keys, weight_grad, input_grad, new_base, new_momentum)


def solution(mesh):
    placed = (
        P(("rep", "fsdp"), None),
        P(),
        P("rep", "fsdp", None),
        P(("rep", "fsdp"), None),
        P("fsdp", None),
        P("rep", "fsdp", None),
        P("fsdp", None),
        P("fsdp"),
        P("rep", "fsdp"),
        P(),
    )
    return jax.shard_map(
        per_device,
        mesh=mesh,
        in_specs=placed,
        out_specs=(
            P(("rep", "fsdp"), None),
            P("rep", "fsdp", None),
            P(("rep", "fsdp"), None),
            P("fsdp", None),
            P("fsdp", None),
        ),
        check_vma=False,
    )
```

```python
import functools

import jax
import jax.numpy as jnp
from jax import lax
from jax.experimental import pallas as pl
from jax.experimental.pallas import tpu as pltpu
from jax.sharding import PartitionSpec as P

eps_norm = 1e-05
momentum_keep = 0.9
outer_rate = 0.7
axes = ("rep", "fsdp")
f32 = jnp.float32
bf16 = jnp.bfloat16
cuts = (0, 1536, 2048)
small = pl.CostEstimate(flops=1024, bytes_accessed=1024, transcendentals=0)


def flip(bit):
    return [(i, i ^ bit) for i in range(256)]


core_bit, x_lo_bit, x_hi_bit, y_bit, z_bit = 1, 2, 4, 8, 32


def send(value, bit):
    return lax.ppermute(value, axes, flip(bit))


def params(limit=58):
    return pltpu.CompilerParams(vmem_limit_bytes=limit * 1024 * 1024)


def level_table(exponents):
    powers = jnp.arange(-6, -1, dtype=jnp.int32)
    values = jnp.array([64.0, 32.0, 16.0, 8.0, 4.0], dtype=jnp.float32)
    match = exponents[:, None] == powers[None, :]
    return jnp.sum(jnp.where(match, values[None, :], jnp.float32(0.0)), axis=1)


def dither_levels(seeds, fragment, lanes):
    lane = jnp.arange(lanes, dtype=jnp.int32)
    first = (seeds[:, None] + 7919 * lane[None, :] + 4099 * fragment) % 32749
    second = (first * first + 3 * first + 17) % 32749
    return second % 16


def norm_kernel(me_ref, x_ref, gain_ref, near_ref, f0_ref, f1_ref, f2_ref, f3_ref, inv_ref):
    width = x_ref.shape[1]
    slab = width // 4
    half = slab // 2
    total = jnp.zeros((x_ref.shape[0], 1), f32)
    for s in range(4):
        part = x_ref[:, s * slab : (s + 1) * slab].astype(f32)
        total = total + jnp.sum(part * part, axis=1, keepdims=True)
    inv = lax.rsqrt(total / width + eps_norm)
    inv_ref[...] = jnp.broadcast_to(inv, inv_ref.shape)
    me = me_ref[0]

    def normed(bits, offset, count):
        col = pl.multiple_of((me ^ bits) * slab + offset, half)
        part = x_ref[:, pl.ds(col, count)].astype(f32)
        return (part * inv * gain_ref[:, pl.ds(col, count)]).astype(bf16)

    near_ref[0] = normed(0, 0, slab)
    near_ref[1] = normed(2, 0, slab)
    f0_ref[...] = normed(1, 0, half)
    f1_ref[...] = normed(1, half, half)
    f2_ref[...] = normed(3, 0, half)
    f3_ref[...] = normed(3, half, half)


def norm_slabs(me, hidden, gain):
    rows, width = hidden.shape
    block = 64
    slab = width // 4
    near, *far, inv = pl.pallas_call(
        norm_kernel,
        grid_spec=pltpu.PrefetchScalarGridSpec(
            num_scalar_prefetch=1,
            grid=(rows // block,),
            in_specs=[
                pl.BlockSpec((block, width), lambda i, m: (i, 0)),
                pl.BlockSpec((1, width), lambda i, m: (0, 0)),
            ],
            out_specs=[pl.BlockSpec((2, block, slab), lambda i, m: (0, i, 0))]
            + [pl.BlockSpec((block, slab // 2), lambda i, m: (i, 0))] * 4
            + [pl.BlockSpec((block, 128), lambda i, m: (i, 0))],
        ),
        out_shape=[pltpu.HBM((2, rows, slab), bf16)]
        + [pltpu.HBM((rows, slab // 2), bf16)] * 4
        + [jax.ShapeDtypeStruct((rows, 128), f32)],
        compiler_params=params(),
        cost_estimate=small,
        name="norm",
    )(me, hidden, gain)
    return near, far, inv


def grad_kernel(mine_ref, low_ref, high_ref, cot_ref, cot_theirs_ref, *out_refs):
    over_tokens = (((0,), (0,)), ((), ()))
    step = 512
    half = low_ref.shape[1]
    for first, last, out_ref in zip(cuts, cuts[1:], out_refs):
        for row in range(first, last, step):
            theirs_ref = low_ref if row < half else high_ref
            a = mine_ref[0, :, row : row + step]
            b = theirs_ref[:, row % half : row % half + step]
            value = lax.dot_general(a, cot_ref[...], over_tokens, preferred_element_type=f32)
            value = value + lax.dot_general(b, cot_theirs_ref[...], over_tokens, preferred_element_type=f32)
            out_ref[row - first : row - first + step, :] = value.astype(out_ref.dtype)


def grad_rows(mine, theirs, cot, cot_theirs, place, dtype, name):
    _, tokens, slab = mine.shape
    width = cot.shape[1]
    counts = [b - a for a, b in zip(cuts, cuts[1:])]
    fixed = lambda i: (0, 0)
    return pl.pallas_call(
        grad_kernel,
        grid=(1,),
        in_specs=[
            pl.BlockSpec((1, tokens, slab), lambda i: (place, 0, 0)),
            pl.BlockSpec((tokens, slab // 2), fixed),
            pl.BlockSpec((tokens, slab // 2), fixed),
            pl.BlockSpec((tokens, width), fixed),
            pl.BlockSpec((tokens, width), fixed),
        ],
        out_specs=[pl.BlockSpec((rows, width), fixed) for rows in counts],
        out_shape=[pltpu.HBM((rows, width), dtype) for rows in counts],
        compiler_params=params(),
        cost_estimate=small,
        name=name,
    )(mine, theirs[2 * place], theirs[2 * place + 1], cot, cot_theirs)


def add_kernel(own_ref, came_ref, *refs):
    refs[-1][0] = (own_ref[...] + came_ref[...].astype(f32)).astype(bf16)


def add_rows(own, came, first, so_far):
    rows, width = own.shape
    block = 512
    part = pl.BlockSpec((block, width), lambda g: (g, 0))
    args = (own, came) if so_far is None else (own, came, so_far)
    return pl.pallas_call(
        add_kernel,
        grid=(rows // block,),
        in_specs=[part, part] + ([] if so_far is None else [pl.BlockSpec(memory_space=pl.ANY)]),
        out_specs=pl.BlockSpec((1, block, width), lambda g: (0, first // block + g, 0)),
        out_shape=jax.ShapeDtypeStruct((1, cuts[-1], width), bf16),
        input_output_aliases={} if so_far is None else {2: 0},
        compiler_params=params(8),
        cost_estimate=small,
        name="add",
    )(*args)


pieces = 4


def token_kernel(me_ref, *refs):
    whole_hbm = refs[:3]
    piece_hbm = refs[3 : 3 + pieces]
    x_hbm, gain_ref, cot_ref, inv_ref, keys_ref, out_hbm = refs[3 + pieces : 9 + pieces]
    w, x, out, sems, out_sems = refs[9 + pieces :]
    _, tokens, slab = x.shape
    half = slab // 2
    width = 4 * slab
    me = me_ref[0]
    used = []

    def load(source, target):
        copy = pltpu.make_async_copy(source, target, sems.at[len(used)])
        used.append(copy)
        copy.start()
        return copy

    def column(s, h):
        return pl.multiple_of((me ^ s) * slab + h * half, half)

    x_waits = []
    w_waits = []
    for s in range(4):
        x_waits.append(load(x_hbm.at[:, pl.ds(column(s, 0), slab)], x.at[s]))
        if s < 3:
            w_waits.append([load(whole_hbm[s], w.at[s])])
        else:
            rows = slab // pieces
            w_waits.append(
                [load(piece_hbm[k], w.at[s, pl.ds(k * rows, rows)]) for k in range(pieces)]
            )

    inv = inv_ref[:, :1]
    keys = jnp.zeros(keys_ref.shape, f32)
    for s in range(4):
        x_waits[s].wait()
        for copy in w_waits[s]:
            copy.wait()
        for h in range(2):
            values = x[s, :, h * half : (h + 1) * half].astype(f32)
            normed = (values * inv * gain_ref[:, pl.ds(column(s, h), half)]).astype(bf16)
            part = w[s, h * half : (h + 1) * half, :]
            keys = keys + jnp.dot(normed, part, preferred_element_type=f32)
    keys_ref[...] = keys.astype(bf16)
    cot = cot_ref[...]
    factor = inv * inv * (jnp.sum(cot.astype(f32) * keys, axis=1, keepdims=True) / width)

    sent = []
    for s in range(4):
        for h in range(2):
            part = w[s, h * half : (h + 1) * half, :]
            dnormed = lax.dot_general(cot, part, (((1,), (1,)), ((), ())), preferred_element_type=f32)
            scaled = gain_ref[:, pl.ds(column(s, h), half)] * dnormed
            values = x[s, :, h * half : (h + 1) * half].astype(f32)
            out[s, h] = (inv * scaled - values * factor).astype(bf16)
            copy = pltpu.make_async_copy(
                out.at[s, h], out_hbm.at[:, pl.ds(column(s, h), half)], out_sems.at[2 * s + h]
            )
            copy.start()
            sent.append(copy)
    for copy in sent:
        copy.wait()


def token_outputs(me, whole, parts, hidden, gain, cot, inv):
    tokens, width = hidden.shape
    slab = width // 4
    keys_width = cot.shape[1]
    far_off = pl.BlockSpec(memory_space=pl.ANY)
    close = pl.BlockSpec(memory_space=pltpu.VMEM)
    return pl.pallas_call(
        token_kernel,
        in_specs=[pl.BlockSpec(memory_space=pltpu.SMEM)] + [far_off] * (4 + pieces) + [close] * 3,
        out_specs=[close, far_off],
        out_shape=[
            jax.ShapeDtypeStruct((tokens, keys_width), bf16),
            jax.ShapeDtypeStruct((tokens, width), bf16),
        ],
        scratch_shapes=[
            pltpu.VMEM((4, slab, keys_width), bf16),
            pltpu.VMEM((4, tokens, slab), bf16),
            pltpu.VMEM((4, 2, tokens, slab // 2), bf16),
            pltpu.SemaphoreType.DMA((7 + pieces,)),
            pltpu.SemaphoreType.DMA((8,)),
        ],
        compiler_params=params(),
        cost_estimate=small,
        name="keys_and_input_grad",
    )(me, *whole, *parts, hidden, gain, cot, inv)


def packed_codes(global_base, replica_params, level, dither_seeds, fragment_index):
    rows_here, lanes = global_base.shape
    third = rows_here // 3
    delta = global_base - replica_params[0].astype(f32)
    offset = (dither_levels(dither_seeds[0], fragment_index[0], lanes).astype(f32) + 0.5) / 16.0
    code = jnp.clip(jnp.floor(delta * level + offset), -8.0, 7.0).astype(jnp.int32)
    shifted = code + 8
    return shifted[:third] + 1024 * shifted[third : 2 * third] + 1048576 * shifted[2 * third :]


def beside(got, work):
    return lax.optimization_barrier((got, work))


def halve(total, step, work):
    z = lax.axis_index("rep") // 8
    half = total.shape[0] // 2
    side = (z // step) % 2
    kept = lax.dynamic_slice_in_dim(total, side * half, half, 0)
    sent = lax.dynamic_slice_in_dim(total, (1 - side) * half, half, 0)
    got, done = beside(send(sent, z_bit * step), work())
    return kept + got, done


def exchange(total, mask, work):
    got, done = beside(send(total, mask), work())
    return total + got, done


def scatter_y(total, work):
    y = (lax.axis_index("rep") // 2) % 4
    quarter = total.shape[0] // 4

    def part(k):
        return lax.dynamic_slice_in_dim(total, (y ^ k) * quarter, quarter, 0)

    got, done = beside([send(part(k), y_bit * k) for k in (1, 2, 3)], work())
    return sum(got, part(0)), done


def in_order(low, mine, other):
    return jnp.where(
        low, jnp.concatenate([mine, other], axis=0), jnp.concatenate([other, mine], axis=0)
    )


def gather_y(total, work):
    y = (lax.axis_index("rep") // 2) % 4
    got, done = beside([send(total, y_bit * k) for k in (1, 2, 3)], work())
    even = y % 2 == 0
    return in_order(y < 2, in_order(even, total, got[0]), in_order(even, got[1], got[2])), done


def gather_z(total, step, work):
    z = lax.axis_index("rep") // 8
    other, done = beside(send(total, z_bit * step), work())
    return in_order((z // step) % 2 == 0, total, other), done


def outer_update(total, global_base, outer_momentum, level, replicas):
    step_size = 1.0 / level
    field_low = total & 1023
    field_mid = (total >> 10) & 1023
    field_high = total >> 20
    code_sum = jnp.concatenate([field_low, field_mid, field_high], axis=0) - 8 * replicas
    outer_grad = code_sum.astype(f32) * (step_size / replicas)
    new_momentum = momentum_keep * outer_momentum + outer_grad
    new_base = global_base - outer_rate * (outer_grad + momentum_keep * new_momentum)
    return (new_base, new_momentum)


def per_device(
    hidden_in,
    norm_gain,
    key_weight,
    key_cot,
    global_base,
    replica_params,
    outer_momentum,
    scale_exponents,
    dither_seeds,
    fragment_index,
):
    me = lax.axis_index("fsdp").astype(jnp.int32)[None]
    gain = norm_gain[None, :]
    own = key_weight[0]
    partner = send(own, x_lo_bit)
    sibling = send(own, core_bit)
    cot_sibling = send(key_cot, core_bit)
    nothing = lambda: ()

    level = level_table(scale_exponents)[:, None]
    total = packed_codes(global_base, replica_params, level, dither_seeds, fragment_index)
    total, hidden = lax.optimization_barrier((total, hidden_in))
    total, (near, far, inv) = halve(total, 4, lambda: norm_slabs(me, hidden, gain))
    total, came = halve(total, 2, lambda: [send(part, core_bit) for part in far])
    total, out_rows = scatter_y(
        total, lambda: grad_rows(near, came, key_cot, cot_sibling, 1, bf16, "grad_out")
    )
    in_rows = [send(rows, x_lo_bit) for rows in out_rows]
    total, own_rows = exchange(
        total,
        x_hi_bit | z_bit,
        lambda: grad_rows(near, came, key_cot, cot_sibling, 0, f32, "grad_own"),
    )
    total, _ = exchange(total, z_bit, nothing)
    total, partner = lax.optimization_barrier((total, partner))
    quarter = partner.shape[0] // pieces
    diagonal = [send(partner[k * quarter : (k + 1) * quarter], core_bit) for k in range(pieces)]
    total, _ = gather_y(total, nothing)
    total, diagonal = gather_z(total, 2, lambda: diagonal)
    total, (keys, input_grad) = gather_z(
        total,
        4,
        lambda: token_outputs(
            me, (own, sibling, partner), diagonal, hidden, gain, key_cot, inv
        ),
    )
    input_grad, in_rows[0] = lax.optimization_barrier((input_grad, in_rows[0]))
    new_base, new_momentum = outer_update(
        total, global_base, outer_momentum, level, lax.axis_size("rep")
    )
    weight_grad = None
    for first, own_part, in_part in zip(cuts, own_rows, in_rows):
        weight_grad = add_rows(own_part, in_part, first, weight_grad)
    return (keys, weight_grad, input_grad, new_base, new_momentum)


def solution(mesh):
    placed = (
        P(("rep", "fsdp"), None),
        P(),
        P("rep", "fsdp", None),
        P(("rep", "fsdp"), None),
        P("fsdp", None),
        P("rep", "fsdp", None),
        P("fsdp", None),
        P("fsdp"),
        P("rep", "fsdp"),
        P(),
    )
    return jax.shard_map(
        per_device,
        mesh=mesh,
        in_specs=placed,
        out_specs=(
            P(("rep", "fsdp"), None),
            P("rep", "fsdp", None),
            P(("rep", "fsdp"), None),
            P("fsdp", None),
            P("fsdp", None),
        ),
        check_vma=False,
    )
```

```python
import functools

import jax
import jax.numpy as jnp
from jax import lax
from jax.experimental import pallas as pl
from jax.experimental.pallas import tpu as pltpu
from jax.sharding import PartitionSpec as P

eps_norm = 1e-05
momentum_keep = 0.9
outer_rate = 0.7
axes = ("rep", "fsdp")
f32 = jnp.float32
bf16 = jnp.bfloat16
cuts = (0, 1536, 2048)
small = pl.CostEstimate(flops=1024, bytes_accessed=1024, transcendentals=0)


def flip(bit):
    return [(i, i ^ bit) for i in range(256)]


core_bit, x_lo_bit, x_hi_bit, y_bit, z_bit = 1, 2, 4, 8, 32


def send(value, bit):
    return lax.ppermute(value, axes, flip(bit))


def params(limit=58):
    return pltpu.CompilerParams(vmem_limit_bytes=limit * 1024 * 1024)


def level_table(exponents):
    powers = jnp.arange(-6, -1, dtype=jnp.int32)
    values = jnp.array([64.0, 32.0, 16.0, 8.0, 4.0], dtype=jnp.float32)
    match = exponents[:, None] == powers[None, :]
    return jnp.sum(jnp.where(match, values[None, :], jnp.float32(0.0)), axis=1)


prime = 32749


def dither_levels(seeds, fragment, lanes):
    lane = (7919 * jnp.arange(lanes, dtype=jnp.int32)) % prime
    row = (seeds + 4099 * fragment) % prime
    first = row[:, None] + lane[None, :]
    first = jnp.where(first >= prime, first - prime, first)
    square = first * (first + 3) + 17
    second = square - (square.astype(f32) * (1.0 / prime)).astype(jnp.int32) * prime
    second = jnp.where(second < 0, second + prime, second)
    second = jnp.where(second >= prime, second - prime, second)
    return second & 15


def norm_kernel(me_ref, x_ref, gain_ref, near_ref, f0_ref, f1_ref, f2_ref, f3_ref, inv_ref):
    width = x_ref.shape[1]
    slab = width // 4
    half = slab // 2
    total = jnp.zeros((x_ref.shape[0], 1), f32)
    for s in range(4):
        part = x_ref[:, s * slab : (s + 1) * slab].astype(f32)
        total = total + jnp.sum(part * part, axis=1, keepdims=True)
    inv = lax.rsqrt(total / width + eps_norm)
    inv_ref[...] = jnp.broadcast_to(inv, inv_ref.shape)
    me = me_ref[0]

    def normed(bits, offset, count):
        col = pl.multiple_of((me ^ bits) * slab + offset, half)
        part = x_ref[:, pl.ds(col, count)].astype(f32)
        return (part * inv * gain_ref[:, pl.ds(col, count)]).astype(bf16)

    near_ref[0] = normed(0, 0, slab)
    near_ref[1] = normed(2, 0, slab)
    f0_ref[...] = normed(1, 0, half)
    f1_ref[...] = normed(1, half, half)
    f2_ref[...] = normed(3, 0, half)
    f3_ref[...] = normed(3, half, half)


def norm_slabs(me, hidden, gain):
    rows, width = hidden.shape
    block = 64
    slab = width // 4
    near, *far, inv = pl.pallas_call(
        norm_kernel,
        grid_spec=pltpu.PrefetchScalarGridSpec(
            num_scalar_prefetch=1,
            grid=(rows // block,),
            in_specs=[
                pl.BlockSpec((block, width), lambda i, m: (i, 0)),
                pl.BlockSpec((1, width), lambda i, m: (0, 0)),
            ],
            out_specs=[pl.BlockSpec((2, block, slab), lambda i, m: (0, i, 0))]
            + [pl.BlockSpec((block, slab // 2), lambda i, m: (i, 0))] * 4
            + [pl.BlockSpec((block, 128), lambda i, m: (i, 0))],
        ),
        out_shape=[pltpu.HBM((2, rows, slab), bf16)]
        + [pltpu.HBM((rows, slab // 2), bf16)] * 4
        + [jax.ShapeDtypeStruct((rows, 128), f32)],
        compiler_params=params(24),
        cost_estimate=small,
        name="norm",
    )(me, hidden, gain)
    return near, far, inv


def grad_kernel(mine_ref, low_ref, high_ref, cot_ref, cot_theirs_ref, *out_refs):
    over_tokens = (((0,), (0,)), ((), ()))
    step = 512
    half = low_ref.shape[1]
    for first, last, out_ref in zip(cuts, cuts[1:], out_refs):
        for row in range(first, last, step):
            theirs_ref = low_ref if row < half else high_ref
            a = mine_ref[0, :, row : row + step]
            b = theirs_ref[:, row % half : row % half + step]
            value = lax.dot_general(a, cot_ref[...], over_tokens, preferred_element_type=f32)
            value = value + lax.dot_general(b, cot_theirs_ref[...], over_tokens, preferred_element_type=f32)
            out_ref[row - first : row - first + step, :] = value.astype(out_ref.dtype)


def grad_rows(mine, theirs, cot, cot_theirs, place, dtype, name):
    _, tokens, slab = mine.shape
    width = cot.shape[1]
    counts = [b - a for a, b in zip(cuts, cuts[1:])]
    fixed = lambda i: (0, 0)
    return pl.pallas_call(
        grad_kernel,
        grid=(1,),
        in_specs=[
            pl.BlockSpec((1, tokens, slab), lambda i: (place, 0, 0)),
            pl.BlockSpec((tokens, slab // 2), fixed),
            pl.BlockSpec((tokens, slab // 2), fixed),
            pl.BlockSpec((tokens, width), fixed),
            pl.BlockSpec((tokens, width), fixed),
        ],
        out_specs=[pl.BlockSpec((rows, width), fixed) for rows in counts],
        out_shape=[jax.ShapeDtypeStruct((rows, width), dtype) for rows in counts],
        compiler_params=params(24),
        cost_estimate=small,
        name=name,
    )(mine, theirs[2 * place], theirs[2 * place + 1], cot, cot_theirs)


def add_kernel(own_ref, came_ref, *refs):
    refs[-1][0] = (own_ref[...] + came_ref[...].astype(f32)).astype(bf16)


def add_rows(own, came, first, so_far):
    rows, width = own.shape
    block = 512
    part = pl.BlockSpec((block, width), lambda g: (g, 0))
    args = (own, came) if so_far is None else (own, came, so_far)
    return pl.pallas_call(
        add_kernel,
        grid=(rows // block,),
        in_specs=[part, part] + ([] if so_far is None else [pl.BlockSpec(memory_space=pl.ANY)]),
        out_specs=pl.BlockSpec((1, block, width), lambda g: (0, first // block + g, 0)),
        out_shape=jax.ShapeDtypeStruct((1, cuts[-1], width), bf16),
        input_output_aliases={} if so_far is None else {2: 0},
        compiler_params=params(8),
        cost_estimate=small,
        name="add",
    )(*args)


pieces = 4


def token_kernel(me_ref, *refs):
    whole_hbm = refs[:3]
    piece_hbm = refs[3 : 3 + pieces]
    x_hbm, gain_ref, cot_ref, inv_ref, keys_ref, out_hbm = refs[3 + pieces : 9 + pieces]
    w, x, out, sems, out_sems = refs[9 + pieces :]
    _, tokens, slab = x.shape
    half = slab // 2
    width = 4 * slab
    me = me_ref[0]
    used = []

    def load(source, target):
        copy = pltpu.make_async_copy(source, target, sems.at[len(used)])
        used.append(copy)
        copy.start()
        return copy

    def column(s, h):
        return pl.multiple_of((me ^ s) * slab + h * half, half)

    x_waits = []
    w_waits = []
    for s in range(4):
        x_waits.append(load(x_hbm.at[:, pl.ds(column(s, 0), slab)], x.at[s]))
        if s < 3:
            w_waits.append([load(whole_hbm[s], w.at[s])])
        else:
            rows = slab // pieces
            w_waits.append(
                [load(piece_hbm[k], w.at[s, pl.ds(k * rows, rows)]) for k in range(pieces)]
            )

    inv = inv_ref[:, :1]
    keys = jnp.zeros(keys_ref.shape, f32)
    for s in range(4):
        x_waits[s].wait()
        for copy in w_waits[s]:
            copy.wait()
        for h in range(2):
            values = x[s, :, h * half : (h + 1) * half].astype(f32)
            normed = (values * inv * gain_ref[:, pl.ds(column(s, h), half)]).astype(bf16)
            part = w[s, h * half : (h + 1) * half, :]
            keys = keys + jnp.dot(normed, part, preferred_element_type=f32)
    keys_ref[...] = keys.astype(bf16)
    cot = cot_ref[...]
    factor = inv * inv * (jnp.sum(cot.astype(f32) * keys, axis=1, keepdims=True) / width)

    sent = []
    for s in range(4):
        for h in range(2):
            part = w[s, h * half : (h + 1) * half, :]
            dnormed = lax.dot_general(cot, part, (((1,), (1,)), ((), ())), preferred_element_type=f32)
            scaled = gain_ref[:, pl.ds(column(s, h), half)] * dnormed
            values = x[s, :, h * half : (h + 1) * half].astype(f32)
            out[s, h] = (inv * scaled - values * factor).astype(bf16)
            copy = pltpu.make_async_copy(
                out.at[s, h], out_hbm.at[:, pl.ds(column(s, h), half)], out_sems.at[2 * s + h]
            )
            copy.start()
            sent.append(copy)
    for copy in sent:
        copy.wait()


def token_outputs(me, whole, parts, hidden, gain, cot, inv):
    tokens, width = hidden.shape
    slab = width // 4
    keys_width = cot.shape[1]
    far_off = pl.BlockSpec(memory_space=pl.ANY)
    close = pl.BlockSpec(memory_space=pltpu.VMEM)
    return pl.pallas_call(
        token_kernel,
        in_specs=[pl.BlockSpec(memory_space=pltpu.SMEM)] + [far_off] * (4 + pieces) + [close] * 3,
        out_specs=[close, far_off],
        out_shape=[
            jax.ShapeDtypeStruct((tokens, keys_width), bf16),
            jax.ShapeDtypeStruct((tokens, width), bf16),
        ],
        scratch_shapes=[
            pltpu.VMEM((4, slab, keys_width), bf16),
            pltpu.VMEM((4, tokens, slab), bf16),
            pltpu.VMEM((4, 2, tokens, slab // 2), bf16),
            pltpu.SemaphoreType.DMA((7 + pieces,)),
            pltpu.SemaphoreType.DMA((8,)),
        ],
        compiler_params=params(40),
        cost_estimate=small,
        name="keys_and_input_grad",
    )(me, *whole, *parts, hidden, gain, cot, inv)


def packed_codes(global_base, replica_params, level, dither_seeds, fragment_index):
    rows_here, lanes = global_base.shape
    third = rows_here // 3
    delta = global_base - replica_params[0].astype(f32)
    offset = (dither_levels(dither_seeds[0], fragment_index[0], lanes).astype(f32) + 0.5) / 16.0
    code = jnp.clip(jnp.floor(delta * level + offset), -8.0, 7.0).astype(jnp.int32)
    shifted = code + 8
    return shifted[:third] + 1024 * shifted[third : 2 * third] + 1048576 * shifted[2 * third :]


def beside(got, work):
    return lax.optimization_barrier((got, work))


def halve(total, step, work):
    z = lax.axis_index("rep") // 8
    half = total.shape[0] // 2
    side = (z // step) % 2
    kept = lax.dynamic_slice_in_dim(total, side * half, half, 0)
    sent = lax.dynamic_slice_in_dim(total, (1 - side) * half, half, 0)
    got, done = beside(send(sent, z_bit * step), work())
    return kept + got, done


def exchange(total, mask, work):
    got, done = beside(send(total, mask), work())
    return total + got, done


def scatter_y(total, work):
    y = (lax.axis_index("rep") // 2) % 4
    quarter = total.shape[0] // 4

    def part(k):
        return lax.dynamic_slice_in_dim(total, (y ^ k) * quarter, quarter, 0)

    got, done = beside([send(part(k), y_bit * k) for k in (1, 2, 3)], work())
    return sum(got, part(0)), done


def in_order(low, mine, other):
    return jnp.where(
        low, jnp.concatenate([mine, other], axis=0), jnp.concatenate([other, mine], axis=0)
    )


def gather_y(total, work):
    y = (lax.axis_index("rep") // 2) % 4
    got, done = beside([send(total, y_bit * k) for k in (1, 2, 3)], work())
    even = y % 2 == 0
    return in_order(y < 2, in_order(even, total, got[0]), in_order(even, got[1], got[2])), done


def gather_z(total, step, work):
    z = lax.axis_index("rep") // 8
    other, done = beside(send(total, z_bit * step), work())
    return in_order((z // step) % 2 == 0, total, other), done


def outer_update(total, global_base, outer_momentum, level, replicas):
    step_size = 1.0 / level
    field_low = total & 1023
    field_mid = (total >> 10) & 1023
    field_high = total >> 20
    code_sum = jnp.concatenate([field_low, field_mid, field_high], axis=0) - 8 * replicas
    outer_grad = code_sum.astype(f32) * (step_size / replicas)
    new_momentum = momentum_keep * outer_momentum + outer_grad
    new_base = global_base - outer_rate * (outer_grad + momentum_keep * new_momentum)
    return (new_base, new_momentum)


def per_device(
    hidden_in,
    norm_gain,
    key_weight,
    key_cot,
    global_base,
    replica_params,
    outer_momentum,
    scale_exponents,
    dither_seeds,
    fragment_index,
):
    me = lax.axis_index("fsdp").astype(jnp.int32)[None]
    gain = norm_gain[None, :]
    own = key_weight[0]
    partner = send(own, x_lo_bit)
    sibling = send(own, core_bit)
    cot_sibling = send(key_cot, core_bit)
    nothing = lambda: ()

    level = level_table(scale_exponents)[:, None]
    total = packed_codes(global_base, replica_params, level, dither_seeds, fragment_index)
    total, hidden = lax.optimization_barrier((total, hidden_in))
    total, (near, far, inv) = halve(total, 2, lambda: norm_slabs(me, hidden, gain))
    total, came = scatter_y(total, lambda: [send(part, core_bit) for part in far])
    total, out_rows = exchange(
        total,
        x_hi_bit | z_bit,
        lambda: grad_rows(near, came, key_cot, cot_sibling, 1, bf16, "grad_out"),
    )
    in_rows = [send(rows, x_lo_bit) for rows in out_rows]
    total, _ = exchange(total, z_bit, nothing)
    total, _ = exchange(total, z_bit * 4, nothing)
    total, partner = lax.optimization_barrier((total, partner))
    quarter = partner.shape[0] // pieces
    diagonal = [send(partner[k * quarter : (k + 1) * quarter], core_bit) for k in range(pieces)]
    total, (diagonal, own_rows) = gather_y(
        total,
        lambda: (diagonal, grad_rows(near, came, key_cot, cot_sibling, 0, f32, "grad_own")),
    )
    total, (keys, input_grad) = gather_z(
        total,
        2,
        lambda: token_outputs(
            me, (own, sibling, partner), diagonal, hidden, gain, key_cot, inv
        ),
    )
    input_grad, in_rows[0] = lax.optimization_barrier((input_grad, in_rows[0]))
    new_base, new_momentum = outer_update(
        total, global_base, outer_momentum, level, lax.axis_size("rep")
    )
    weight_grad = None
    for first, own_part, in_part in zip(cuts, own_rows, in_rows):
        weight_grad = add_rows(own_part, in_part, first, weight_grad)
    return (keys, weight_grad, input_grad, new_base, new_momentum)


def solution(mesh):
    placed = (
        P(("rep", "fsdp"), None),
        P(),
        P("rep", "fsdp", None),
        P(("rep", "fsdp"), None),
        P("fsdp", None),
        P("rep", "fsdp", None),
        P("fsdp", None),
        P("fsdp"),
        P("rep", "fsdp"),
        P(),
    )
    return jax.shard_map(
        per_device,
        mesh=mesh,
        in_specs=placed,
        out_specs=(
            P(("rep", "fsdp"), None),
            P("rep", "fsdp", None),
            P(("rep", "fsdp"), None),
            P("fsdp", None),
            P("fsdp", None),
        ),
        check_vma=False,
    )
```
